32 devices in a mesh: grp: 2 (over x), lon: 16 (over z, y, core).
Axes of the slice: x: 2, y: 2, z: 4, core: 2. Of those that a mesh axis runs over, the one named last changes fastest.
Arguments:
- tokens: bfloat16 [8, 48, 192, 192], P('grp', None, 'lon'), parts along dimension 0, may hold values from -6 to 6
- qkv_weight: bfloat16 [192, 576], replicated, may hold values from -25 to 25
- proj_weight: bfloat16 [192, 192], replicated, may hold values from -0.4375 to 0.4375
- bias_table: float32 [16, 6, 3312], replicated, may hold values from -4 to 4
- bias_index: int32 [144, 144], replicated, may hold values from 0 to 3311, as said below
- norm_gain1: float32 [192], replicated, may hold values from 0.1 to 1.9
- norm_gain2: float32 [192], replicated, may hold values from 0.1 to 1.9
- mlp_in: bfloat16 [192, 768], replicated, may hold values from -0.4375 to 0.4375
- mlp_out: bfloat16 [768, 192], replicated, may hold values from -0.21875 to 0.21875
Outputs:
- block_out: bfloat16 [8, 48, 192, 192], P('grp', None, 'lon'), parts along dimension 0
The draws below stay inside these ranges and needn't reach their ends.
There are 2 independent parts, one for each index of `grp`. The reference program is written for one: setup_inputs(seed, part) draws one part's arguments, and reference() takes and returns one part's arrays. A program takes and returns all parts, laid end to end along the dimension named above; an argument that names none is the same for every part. Nothing has to cross between parts.
Inputs may be any that keep to these rules, and one draw needn't show every extreme that they name: bias_index[i, j] is the bias table's row for query position i and key position j; pairs with the same level pair, the same row pair and the same column offset share a row, and every row is used.
All inputs are finite; a program needn't handle non-finite values.
Results may differ from the reference program's by a relative error of at most 0.011.
Values may be sent and summed in bfloat16 or wider, within the bound.
No kernel may reach another device: no remote copies, remote signals or barrier semaphores. Data moves between devices by JAX's collectives and lax.ppermute only.
A program may use at most 256 MiB of HBM per device.

```python
import jax
import jax.numpy as jnp
from jax import lax

WIDTH = 192
HEADS = 6
FFN = 768
LEVELS = 4
LAT = 48
LON = 192
BIAS_ROWS = 3312
WTYPES = 16


def draw_qkv_weight(key, part):
    key = jax.random.fold_in(key, 11)
    initial = jax.random.truncated_normal(key, -4.0, 4.0, (WIDTH, 3 * WIDTH), jnp.float32) * WIDTH ** (-0.5)
    return initial.astype(jnp.bfloat16)


def draw_bias_index(key, part):
    key = jax.random.fold_in(key, 23)
    position = jnp.arange(144, dtype=jnp.int32)
    level_pos = position // 72
    row_pos = position // 12 % 6
    column_pos = position % 12
    pangu_code = ((level_pos[:, None] * 2 + level_pos[None, :]) * 36 + row_pos[:, None] * 6 + row_pos[None, :]) * 23 + column_pos[:, None] - column_pos[None, :] + 11
    shuffle = jax.random.permutation(key, BIAS_ROWS).astype(jnp.int32)
    return shuffle[pangu_code].astype(jnp.int32)


def steps_of(key, dims, split, smallest, largest):
    def one(dim, blocks):
        draws = jax.random.uniform(jax.random.fold_in(jax.random.fold_in(key, 6), dim), (blocks,), jnp.float32, smallest / len(split), largest / len(split))
        return jnp.repeat(jnp.exp(draws), dims[dim] // blocks).reshape((-1,) + (1,) * (len(dims) - dim - 1))

    level = one(*split[0])
    for cut in split[1:]:
        level = level * one(*cut)
    return level


def bell_draw(key, shape, width, limit, cuts=(), kind=jnp.bfloat16):
    drawn = jax.random.normal(key, shape, jnp.float32) * width
    if len(cuts) > 0:
        drawn = steps_of(key, shape, cuts, -0.22, 0.18) * drawn
    return jnp.clip(drawn, min=-limit, max=limit).astype(kind)


def setup_inputs(seed: int = 0, part: int = 0) -> dict:
    keys = jax.random.split(jax.random.key(seed), 10)
    part_keys = jax.random.split(jax.random.fold_in(keys[9], part), 10)
    return {
        "tokens": bell_draw(part_keys[0], (LEVELS, LAT, LON, WIDTH), 1.0, 6.0, ((2, 16),)),
        "qkv_weight": draw_qkv_weight(jax.random.fold_in(keys[9], 71), part),
        "proj_weight": bell_draw(keys[2], (WIDTH, WIDTH), WIDTH ** -0.5, 0.4375),
        "bias_table": bell_draw(keys[3], (WTYPES, HEADS, BIAS_ROWS), 1.0, 4.0, (), jnp.float32),
        "bias_index": draw_bias_index(jax.random.fold_in(keys[9], 71), part),
        "norm_gain1": jnp.clip(1.0 + 0.18 * jax.random.normal(keys[5], (WIDTH,), jnp.float32), 0.1, 1.9),
        "norm_gain2": jnp.clip(1.0 + 0.18 * jax.random.normal(keys[6], (WIDTH,), jnp.float32), 0.1, 1.9),
        "mlp_in": bell_draw(keys[7], (WIDTH, FFN), WIDTH ** -0.5, 0.4375),
        "mlp_out": bell_draw(keys[8], (FFN, WIDTH), FFN ** -0.5, 0.21875),
    }


def region_grid(levels, lat_rows):
    level_ids = jnp.arange(levels, dtype=jnp.int32)
    zone_level = jnp.where(level_ids < levels - 2, 0, jnp.where(level_ids < levels - 1, 1, 2))
    row_ids = jnp.arange(lat_rows, dtype=jnp.int32)
    zone_row = jnp.where(row_ids < lat_rows - 6, 0, jnp.where(row_ids < lat_rows - 3, 1, 2))
    return (zone_level[:, None] * 3 + zone_row[None, :]).astype(jnp.int32)

def to_windows(field_grid, columns):
    levels, lat_rows, longitude, features = field_grid.shape
    window_count = longitude // columns
    pieces = field_grid.reshape(levels // 2, 2, lat_rows // 6, 6, window_count, columns, features)
    return pieces.transpose(0, 2, 4, 1, 3, 5, 6).reshape(levels // 2, lat_rows // 6, window_count, 12 * columns, features)

def from_windows(blocked, columns):
    level_windows, row_windows, window_count, positions, features = blocked.shape
    pieces = blocked.reshape(level_windows, row_windows, window_count, 2, 6, columns, features)
    return pieces.transpose(0, 3, 1, 4, 2, 5, 6).reshape(level_windows * 2, row_windows * 6, window_count * columns, features)

def window_zones(levels, lat_rows, columns):
    zone_ids = region_grid(levels, lat_rows).reshape(levels // 2, 2, lat_rows // 6, 6).transpose(0, 2, 1, 3)
    zone_ids = jnp.broadcast_to(zone_ids[..., None], (levels // 2, lat_rows // 6, 2, 6, columns))
    return zone_ids.reshape(levels // 2, lat_rows // 6, 12 * columns)

def layer_norm(values):
    average = lax.optimization_barrier(jnp.mean(values, axis=-1, keepdims=True))
    centred = values - average
    spread = lax.optimization_barrier(jnp.mean(centred * centred, axis=-1, keepdims=True))
    return centred * lax.rsqrt(spread + 1e-05)

def reference(tokens, qkv_weight, proj_weight, bias_table, bias_index, norm_gain1, norm_gain2, mlp_in, mlp_out):
    levels, lat_rows, longitude, channels = tokens.shape
    head_size = channels // HEADS
    shifted = jnp.roll(tokens, (-1, -3, -6), axis=(0, 1, 2))
    projected = jnp.dot(shifted, qkv_weight, preferred_element_type=jnp.float32).astype(jnp.bfloat16)
    windows = to_windows(projected, 12)
    level_windows, row_windows, window_count = windows.shape[:3]
    windows = windows.reshape(level_windows * row_windows, window_count, 144, 3, HEADS, head_size)
    zone_ids = window_zones(levels, lat_rows, 12).reshape(level_windows * row_windows, 144)

    def one_type(blocked):
        pieces, table_rows, zone_row = blocked
        earth_bias = jnp.take(table_rows, bias_index, axis=1)
        query = pieces[:, :, 0].astype(jnp.float32)
        keyed = pieces[:, :, 1].astype(jnp.float32)
        valued = pieces[:, :, 2].astype(jnp.float32)
        scores = jnp.einsum('nqhd,nkhd->nhqk', query, keyed) * head_size ** (-0.5) + earth_bias[None]
        allowed = zone_row[:, None] == zone_row[None, :]
        scores = jnp.where(allowed[None, None], scores, -1000000000.0)
        highest = lax.optimization_barrier(jnp.max(scores, axis=-1, keepdims=True))
        weights = jnp.exp(scores - highest)
        probabilities = (weights / lax.optimization_barrier(jnp.sum(weights, axis=-1, keepdims=True))).astype(jnp.bfloat16)
        context = jnp.einsum('nhqk,nkhd->nqhd', probabilities.astype(jnp.float32), valued)
        return context.astype(jnp.bfloat16)
    context = lax.map(one_type, (windows, bias_table, zone_ids))
    context = context.reshape(level_windows, row_windows, window_count, 144, channels)
    context = from_windows(context, 12)
    attended = jnp.dot(context, proj_weight, preferred_element_type=jnp.float32).astype(jnp.bfloat16)
    attended = jnp.roll(attended, (1, 3, 6), axis=(0, 1, 2))
    middle = (tokens.astype(jnp.float32) + norm_gain1 * layer_norm(attended.astype(jnp.float32))).astype(jnp.bfloat16)
    expanded = jax.nn.gelu(jnp.dot(middle, mlp_in, preferred_element_type=jnp.float32), approximate=False).astype(jnp.bfloat16)
    reduced = jnp.dot(expanded, mlp_out, preferred_element_type=jnp.float32)
    return (middle.astype(jnp.float32) + norm_gain2 * layer_norm(reduced)).astype(jnp.bfloat16)
```

```python
import functools
import math

import jax
import jax.numpy as jnp
import numpy as np
from jax import lax
from jax.experimental import pallas as pl
from jax.experimental.pallas import tpu as pltpu
from jax.sharding import PartitionSpec as P

LOG2E = math.log2(math.e)
NEG = -1.0e9 * LOG2E
NT = (((1,), (1,)), ((), ()))
NN = (((1,), (0,)), ((), ()))
HEADS = 6
GROUP = 72
LANES = 512
F32 = jnp.float32
BF16 = jnp.bfloat16


def mm(a, b, dims=NN):
    return lax.dot_general(a, b, dims, preferred_element_type=F32)


PAIR_TILES = ((0,), (0, 1), (1, 2), (2, 0))
TILE_PAIRS = ((3, 0, 1), (1, 2), (2, 3))


def pair_rows(pair):
    out = []
    for w in range(2):
        for slot in range(12):
            for r in range(6):
                out.append((slot, (6 * (2 * pair + w) + r + 3) % 48))
    return out


def pack_matrices():
    mats = []
    for pair in range(4):
        tiles = PAIR_TILES[pair]
        m = np.zeros((144, 192 * len(tiles)), np.float32)
        for k, (slot, a) in enumerate(pair_rows(pair)):
            m[k, 192 * tiles.index(a // 16) + slot * 16 + a % 16] = 1.0
        mats.append(m)
    return np.concatenate(mats, axis=1)


def unpack_matrices():
    mats = []
    for tile in range(3):
        pairs = TILE_PAIRS[tile]
        m = np.zeros((192, 144 * len(pairs)), np.float32)
        for n, pair in enumerate(pairs):
            for k, (slot, a) in enumerate(pair_rows(pair)):
                if a // 16 == tile:
                    m[slot * 16 + a % 16, 144 * n + k] = 1.0
        mats.append(np.pad(m, ((0, 0), (0, 432 - m.shape[1]))))
    return np.stack(mats)


def pick_matrix():
    m = np.zeros((GROUP, LANES), np.float32)
    for h in range(HEADS):
        for q in range(GROUP):
            m[q, h * GROUP + q] = 1.0
    return m


def pack_kernel(tok, mats, west, east):
    for wz in range(2):
        zs = ((2 * wz + 1) % 4, (2 * wz + 2) % 4)
        for half, out in ((0, west), (1, east)):
            tiles = []
            for j in range(3):
                tiles.append(
                    jnp.concatenate(
                        [tok[z, 6 * half + c, 16 * j : 16 * j + 16, :] for c in range(6) for z in zs], axis=0
                    )
                )
            at = 0
            for pair in range(4):
                total = None
                for j in PAIR_TILES[pair]:
                    part = mm(mats[:, at : at + 192], tiles[j])
                    total = part if total is None else total + part
                    at += 192
                out[pl.ds((wz * 4 + pair) * 144, 144), :] = total.astype(BF16)


def prep_kernel(tab, idx, bias, tab_t, rows):
    count = tab.shape[1]
    for k in range(0, count, 128):
        n = min(128, count - k)
        tab_t[k : k + n, 0:96] = (tab[:, k : k + n] * LOG2E).T
    lane = lax.broadcasted_iota(jnp.int32, (16, LANES), 1)
    sub = lax.broadcasted_iota(jnp.int32, (16, LANES), 0)
    place = lane % GROUP
    slot = lane % 12
    lq_is1 = slot >= 6
    rq_hi = (slot % 6) >= 3
    last_level = sub >= 8
    last_row = (sub % 8) == 7

    def body(kr, carry):
        j0 = kr * 12
        for m in range(4):
            for c in range(6):
                if m == 0:
                    cq, ck = 0, (12 - c if c else 11)
                elif m == 1:
                    cq, ck = 0, 6 - c
                else:
                    cq, ck = 6 * (m - 2) + c, 0
                for e in range(12):
                    r = idx[e * 12 + cq, j0 + ck]
                    rows[m, c * 12 + e : c * 12 + e + 1, :] = tab_t[pl.ds(r, 1), :]
        xs = []
        for m in range(4):
            t = rows[m].T
            xs.append(
                jnp.concatenate(
                    [t[16 * h : 16 * h + 16, :] for h in range(HEADS)]
                    + [jnp.zeros((16, LANES - HEADS * GROUP), F32)],
                    axis=1,
                )
            )
        prev = [pltpu.roll(x, LANES - GROUP, 1) for x in xs]
        lk_is1 = kr >= 6
        rk_hi = (kr % 6) >= 3
        bad = (last_level & (lq_is1 != lk_is1)) | (last_row & (rq_hi != rk_hi))
        for s in range(2):
            for ck in range(12):
                u, v = divmod(ck, 6)
                m = 3 - s - u
                if v == 0:
                    row = xs[m]
                else:
                    keep = (place < GROUP - 12 * v) & (lane < HEADS * GROUP)
                    row = pltpu.roll(jnp.where(keep, xs[m], prev[m - 1]), 12 * v, 1)
                row = jnp.where(bad, NEG, row)
                for k in range(LANES // 128):
                    bias[k, pl.ds(s * 144 + ck * 12 + kr, 16, stride=288), :] = row[:, 128 * k : 128 * k + 128]
        return carry

    lax.fori_loop(0, 12, body, 0)


def norm(values):
    average = jnp.mean(values, axis=-1, keepdims=True)
    centred = values - average
    spread = jnp.mean(centred * centred, axis=-1, keepdims=True)
    return centred * lax.rsqrt(spread + 1e-05)


def main_kernel(
    own_w, own_e, halo_w, halo_e, bias, wq, wk, wv_t, wp, gain1, gain2, w_in, w_out, pick, unmat, out, done
):
    step = pl.program_id(0)
    wz = step // 4
    pair = step % 4
    channel = lax.broadcasted_iota(jnp.int32, (GROUP, 192), 1)
    lane = lax.broadcasted_iota(jnp.int32, (32, LANES), 1)
    owns, contexts = [], []
    for s in range(2):
        own_ref, halo_ref = ((own_w, halo_w), (own_e, halo_e))[s]
        own = own_ref[...]
        own32 = own.astype(F32)
        halo32 = halo_ref[...].astype(F32)
        owns.append(own32)
        q2 = mm(own, wq[...]) * (LOG2E / math.sqrt(32.0))
        for t in range(2):
            a, b = own32[GROUP * t : GROUP * (t + 1)], halo32[GROUP * t : GROUP * (t + 1)]
            window = jnp.concatenate([b, a] if s == 0 else [a, b], axis=0).astype(BF16)
            keys = mm(window, wk[...]).astype(BF16)
            values_t = mm(wv_t[...], window, NT).astype(BF16)
            values_t = jnp.concatenate([values_t, jnp.ones((16, 144), BF16)], axis=0)
            q = q2[GROUP * t : GROUP * (t + 1)]
            blocks = [
                jnp.where((channel >= 32 * h) & (channel < 32 * h + 32), q, 0.0) for h in range(HEADS)
            ] + [jnp.zeros((LANES - HEADS * GROUP, 192), F32)]
            queries = jnp.concatenate(blocks, axis=0).astype(BF16)
            first = 288 * t + 144 * s
            offset = jnp.concatenate([bias[k, first : first + 144, :] for k in range(LANES // 128)], axis=1)
            scores = mm(keys, queries, NT) + offset
            scores = jnp.where(offset < -1.0e8, NEG, scores)
            highest = jnp.max(scores, axis=0, keepdims=True)
            weights = jnp.exp2(scores - highest).astype(BF16)
            mixed = mm(values_t, weights)
            inverse = 1.0 / mixed[192:193]
            diag = jnp.concatenate(
                [
                    jnp.where(
                        (lane >= GROUP * h) & (lane < GROUP * h + GROUP), mixed[32 * h : 32 * h + 32] * inverse, 0.0
                    )
                    for h in range(HEADS)
                ],
                axis=0,
            ).astype(BF16)
            contexts.append(mm(pick[...], diag, NT))
    context = jnp.concatenate(contexts, axis=0).astype(BF16)
    own32 = jnp.concatenate(owns, axis=0)
    attended = mm(context, wp[...]).astype(BF16).astype(F32)
    middle = (own32 + gain1[...] * norm(attended)).astype(BF16)
    hidden = mm(middle, w_in[...])
    expanded = (0.5 * hidden * (1.0 + lax.erf(hidden * (1.0 / math.sqrt(2.0))))).astype(BF16)
    reduced = mm(expanded, w_out[...])
    result = (middle.astype(F32) + gain2[...] * norm(reduced)).astype(BF16)
    done[0, pl.ds(pl.multiple_of(pair * 144, 144), 144), :] = result[:144]
    done[1, pl.ds(pl.multiple_of(pair * 144, 144), 144), :] = result[144:]

    @pl.when(pair == 3)
    def _():
        for half in range(2):
            for j in range(3):
                pairs = TILE_PAIRS[j]
                if j == 0:
                    rows = jnp.concatenate([done[half, 432:576, :], done[half, 0:288, :]], axis=0)
                else:
                    rows = done[half, 144 * pairs[0] : 144 * pairs[0] + 288, :]
                back = mm(unmat[j, :, : 144 * len(pairs)], rows).astype(BF16)
                for c in range(6):
                    for level in range(2):
                        k = 2 * c + level
                        z = lax.rem(2 * wz + 1 + level, 4)
                        out[z, 6 * half + c, 16 * j : 16 * j + 16, :] = back[16 * k : 16 * k + 16]


def shifted_by(value, axis, steps):
    count = lax.axis_size(axis)
    return lax.ppermute(value, axis, [(i, (i + steps) % count) for i in range(count)])


def per_device(
    tokens, qkv_weight, proj_weight, bias_table, bias_index, norm_gain1, norm_gain2, mlp_in, mlp_out
):
    levels, lat, strip, channels = tokens.shape
    types, heads, count = bias_table.shape
    tok = tokens.transpose(0, 2, 1, 3)
    vmem = pl.BlockSpec(memory_space=pltpu.VMEM)
    half_shape = jax.ShapeDtypeStruct((types * GROUP, channels), BF16)
    west, east = pl.pallas_call(
        pack_kernel,
        out_shape=(half_shape, half_shape),
        in_specs=[vmem, vmem],
        out_specs=(vmem, vmem),
        name="pack",
    )(tok, jnp.asarray(pack_matrices(), BF16))
    halo_w = shifted_by(east, "lon", 1)
    halo_e = shifted_by(west, "lon", -1)
    table = bias_table.transpose(1, 0, 2).reshape(heads * types, count)
    bias = pl.pallas_call(
        prep_kernel,
        out_shape=jax.ShapeDtypeStruct((LANES // 128, types * 288, 128), F32),
        in_specs=[vmem, pl.BlockSpec(memory_space=pltpu.SMEM)],
        out_specs=vmem,
        scratch_shapes=[pltpu.VMEM((3328, 128), F32), pltpu.VMEM((4, GROUP, 128), F32)],
        compiler_params=pltpu.CompilerParams(vmem_limit_bytes=40 * 1024 * 1024),
        cost_estimate=pl.CostEstimate(flops=20_000_000_000, bytes_accessed=12_000_000, transcendentals=0),
        name="bias_prep",
    )(table, bias_index)

    def whole(*shape):
        return pl.BlockSpec(shape, lambda i: (0,) * len(shape))

    strip_spec = pl.BlockSpec((2 * GROUP, channels), lambda i: (i, 0))
    hidden = mlp_in.shape[1]
    out = pl.pallas_call(
        main_kernel,
        grid=(types // 2,),
        out_shape=jax.ShapeDtypeStruct((levels, strip, lat, channels), BF16),
        in_specs=[strip_spec] * 4
        + [
            pl.BlockSpec((LANES // 128, 576, 128), lambda i: (0, i, 0)),
            whole(channels, channels),
            whole(channels, channels),
            whole(channels, channels),
            whole(channels, channels),
            whole(1, channels),
            whole(1, channels),
            whole(channels, hidden),
            whole(hidden, channels),
            whole(GROUP, LANES),
            whole(3, 192, 432),
        ],
        out_specs=whole(levels, strip, lat, channels),
        scratch_shapes=[pltpu.VMEM((2, 576, channels), BF16)],
        compiler_params=pltpu.CompilerParams(vmem_limit_bytes=40 * 1024 * 1024),
        name="block",
    )(
        west,
        east,
        halo_w,
        halo_e,
        bias,
        qkv_weight[:, :channels],
        qkv_weight[:, channels : 2 * channels],
        qkv_weight[:, 2 * channels :].T,
        proj_weight,
        norm_gain1[None],
        norm_gain2[None],
        mlp_in,
        mlp_out,
        jnp.asarray(pick_matrix(), BF16),
        jnp.asarray(unpack_matrices(), BF16),
    )
    return out.transpose(0, 2, 1, 3)


def solution(mesh):
    placed = (P("grp", None, "lon", None), P(), P(), P(), P(), P(), P(), P(), P())
    return jax.shard_map(
        per_device,
        mesh=mesh,
        in_specs=placed,
        out_specs=P("grp", None, "lon", None),
        check_vma=False,
    )
```

```python
import math

import jax
import jax.numpy as jnp
import numpy as np
from jax import lax
from jax.experimental import pallas as pl
from jax.experimental.pallas import tpu as pltpu
from jax.sharding import PartitionSpec as P

LOG2E = math.log2(math.e)
NEG = -1.0e9 * LOG2E
NT = (((1,), (1,)), ((), ()))
NN = (((1,), (0,)), ((), ()))
HEADS = 6
GROUP = 72
TYPES = 4
LANES = 512
F32 = jnp.float32
BF16 = jnp.bfloat16


def mm(a, b, dims=NN):
    return lax.dot_general(a, b, dims, preferred_element_type=F32)


PAIR_TILES = ((0,), (0, 1), (1, 2), (2, 0))
TILE_PAIRS = ((3, 0, 1), (1, 2), (2, 3))


def pair_rows(pair):
    out = []
    for w in range(2):
        for slot in range(12):
            for r in range(6):
                out.append((slot, (6 * (2 * pair + w) + r + 3) % 48))
    return out


def pack_matrices():
    mats = []
    for pair in range(4):
        for tile in PAIR_TILES[pair]:
            m = np.zeros((144, 192), np.float32)
            for k, (slot, a) in enumerate(pair_rows(pair)):
                if a // 16 == tile:
                    m[k, slot * 16 + a % 16] = 1.0
            mats.append(m)
    return np.stack(mats)


def unpack_matrices():
    mats = []
    for tile in range(3):
        pairs = TILE_PAIRS[tile]
        m = np.zeros((192, 144 * len(pairs)), np.float32)
        for n, pair in enumerate(pairs):
            for k, (slot, a) in enumerate(pair_rows(pair)):
                if a // 16 == tile:
                    m[slot * 16 + a % 16, 144 * n + k] = 1.0
        mats.append(np.pad(m, ((0, 0), (0, 432 - m.shape[1]))))
    return np.stack(mats)


def mask_codes():
    lane = np.arange(256)[None] + np.zeros((24, 1), np.int32)
    second = np.arange(24)[:, None] >= 12
    kr = np.arange(24)[:, None] % 12
    slot = (lane % GROUP) % 12
    code = ((slot >= 6) != (kr >= 6)) * 1 + ((slot % 6 >= 3) != (kr % 6 >= 3)) * 2
    source = np.where(second, (lane + 244) % 256, lane)
    place = np.where(source < 3 * GROUP, source % GROUP, GROUP) + 12 * second
    return np.stack([code, place])


def pack_kernel(tok, mats, send_w, send_e):
    for wz in range(2):
        zs = ((2 * wz + 1) % 4, (2 * wz + 2) % 4)
        for half, send in ((0, send_w), (1, send_e)):
            tiles = [
                jnp.concatenate(
                    [tok[z, 6 * half + c, 16 * j : 16 * j + 16, :] for c in range(6) for z in zs], axis=0
                )
                for j in range(3)
            ]
            at = 0
            for pair in range(4):
                total = None
                for j in PAIR_TILES[pair]:
                    part = mm(mats[at], tiles[j])
                    total = part if total is None else total + part
                    at += 1
                piece = total.astype(BF16)
                first = 576 * wz + 144 * pair
                send[first : first + 144, :] = piece[:, :128]
                send[1152 + 144 * pair : 1296 + 144 * pair, 64 * wz : 64 * wz + 64] = piece[:, 128:]


def turn(x, by):
    half = LANES // 2
    if by % half == 0:
        return x
    return jnp.concatenate([pltpu.roll(x[:, k : k + half], by % half, 1) for k in range(0, x.shape[1], half)], axis=1)


def gather_kernel(tab, index, qkv, mlp_out_t, tables, weight, w_out, tab_t, rows, picked, idx, sem):
    numbers = index[...].astype(F32)
    turned = numbers.T
    picked[...] = jnp.concatenate(
        [numbers[12 * e : 12 * e + 1] for e in range(12)] + [turned[12 * e : 12 * e + 1] for e in range(12)], axis=0
    ).astype(jnp.int32)
    copy = pltpu.make_async_copy(picked, idx, sem)
    copy.start()
    w_out[...] = mlp_out_t[...].astype(F32).T.astype(BF16)
    whole = qkv[...].astype(F32)
    gap = jnp.zeros((192, 32), F32)
    cols = []
    for k in range(6):
        cols += [whole[:, 96 * k : 96 * k + 96], gap]
    wide = jnp.concatenate(cols, axis=1).astype(BF16)
    none = jnp.zeros((64, 768), BF16)
    for wz in range(2):
        weight[wz, 0:128, :] = wide[:128]
        weight[wz, 128 + 64 * wz : 192 + 64 * wz, :] = wide[128:]
        weight[wz, 192 - 64 * wz : 256 - 64 * wz, :] = none
    count = tab.shape[1]
    for k in range(0, count, 128):
        n = min(128, count - k)
        tab_t[k : k + n, 0:96] = (tab[:, k : k + n] * LOG2E).T
    copy.wait()
    gap = jnp.zeros((16, 40), F32)
    for kr in range(12):
        j0 = kr * 12
        for m in range(4):
            for c in range(6):
                if m == 0:
                    cq, ck = 0, (12 - c if c else 11)
                elif m == 1:
                    cq, ck = 0, 6 - c
                else:
                    cq, ck = 6 * (m - 2) + c, 0
                for e in range(12):
                    r = idx[e, j0 + ck] if m < 2 else idx[12 + kr, e * 12 + cq]
                    rows[kr, m, c * 12 + e : c * 12 + e + 1, :] = tab_t[pl.ds(r, 1), :]
            t = rows[kr, m].T
            x = jnp.concatenate(
                [t[16 * h : 16 * h + 16, :] for h in range(3)]
                + [gap]
                + [t[16 * h : 16 * h + 16, :] for h in range(3, 6)]
                + [gap],
                axis=1,
            )
            for k in range(LANES // 128):
                tables[m, k, 16 * kr : 16 * kr + 16, :] = x[:, 128 * k : 128 * k + 128]


    def variants(kr, carry):
        here = pl.ds(pl.multiple_of(16 * kr, 16), 16)
        later = pl.ds(pl.multiple_of(192 + 16 * kr, 16), 16)
        for m in range(4):
            x = jnp.concatenate([tables[m, k, here, :] for k in range(LANES // 128)], axis=1)
            moved = turn(x, -GROUP)
            pieces = [(m, later, turn(x, 12))]
            if m < 3:
                pieces += [(4 + m, here, moved), (4 + m, later, turn(moved, 12))]
            for n, at, value in pieces:
                for k in range(LANES // 128):
                    tables[n, k, at, :] = value[:, 128 * k : 128 * k + 128]
        return carry

    lax.fori_loop(0, 12, variants, 0)


def norm(values, eps):
    average = jnp.mean(values, axis=-1, keepdims=True)
    centred = values - average
    spread = jnp.mean(centred * centred, axis=-1, keepdims=True)
    return centred * lax.rsqrt(spread + eps)


def main_kernel(
    send_w, send_e, halo_w, halo_e, tables, codes, weight, wp, gain1, gain2, w_in, w_out, unmat, out, done, held, kept
):
    step = pl.program_id(0)
    steps = 16 // TYPES
    span = TYPES * GROUP
    wz = step * TYPES // 8
    turn_of = step % (8 // TYPES)
    low = pl.ds(pl.multiple_of(step * span, span), span)
    high = pl.ds(pl.multiple_of(1152 + turn_of * span, span), span)
    sides = ((send_w, halo_w), (send_e, halo_e))

    def project():
        channel = lax.broadcasted_iota(jnp.int32, (1, 128), 1)
        scale = LOG2E / math.sqrt(32.0)
        heads = [jnp.where((channel >= 32 * i) & (channel < 32 * i + 32), scale, 0.0) for i in range(3)]
        own, halo = (
            jnp.concatenate([jnp.concatenate([s[k][low, :], s[k][high, :]], axis=1) for s in sides], axis=0)
            for k in range(2)
        )
        return heads, mm(own, weight[wz]), mm(halo, weight[wz, :, 256:])

    def score(heads, own_qkv, halo_kv):
        scores, values = [], []
        ones = jnp.ones((16, 144), BF16)
        for s in range(2):
            for t in range(TYPES):
                at = span * s + GROUP * t
                parts = [own_qkv[at : at + GROUP, 256:], halo_kv[at : at + GROUP]]
                pair_kv = jnp.concatenate(parts[::-1] if s == 0 else parts, axis=0)
                keys = pair_kv[:, :256].astype(BF16)
                turned = pair_kv[:, 256:].T.astype(BF16)
                flags = jnp.where(wz == 1, 1, 0) + (
                    jnp.where(turn_of == 8 // TYPES - 1, 2, 0) if t == TYPES - 1 else 0
                )
                bad = (codes[0] & flags) != 0
                place = codes[1]
                for g in range(2):
                    q = own_qkv[at : at + GROUP, 128 * g : 128 * g + 128]
                    queries = jnp.concatenate([q * heads[i] for i in range(3)] + [jnp.zeros((40, 128), F32)], axis=0)
                    raw = mm(keys[:, 128 * g : 128 * g + 128], queries.astype(BF16), NT)
                    rows = pl.ds(step * TYPES + t, 24, stride=16)
                    table = [
                        jnp.concatenate([tables[m, 2 * g + k, rows, :] for k in range(2)], axis=1)
                        for m in (3 - s, 2 - s, 6 - s, 5 - s)
                    ]
                    chunks = []
                    for c in range(6):
                        u, v = divmod(2 * c, 6)
                        offset = turn(jnp.where(place < GROUP - 12 * v, table[u], table[2 + u]), 12 * v)
                        chunks.append(jnp.where(bad, NEG, raw[24 * c : 24 * c + 24] + offset))
                    scores.append(jnp.concatenate(chunks, axis=0))
                    values.append(jnp.concatenate([turned[128 * g : 128 * g + 96], ones], axis=0))
        return scores, values

    def soften(scores):
        return [jnp.exp2(x - jnp.max(x, axis=0, keepdims=True)).astype(BF16) for x in scores]

    def keep(mixes):
        for n in range(2 * TYPES):
            pieces = []
            for g in range(2):
                mixed = mixes[2 * n + g]
                inverse = 1.0 / mixed[96:97]
                for i in range(3):
                    at = GROUP * i
                    pieces.append(mixed[32 * i : 32 * i + 32, at : at + GROUP] * inverse[:, at : at + GROUP])
            held[GROUP * n : GROUP * n + GROUP, :] = jnp.concatenate(pieces, axis=0).T
        for s in range(2):
            ref = sides[s][0]
            upper = pltpu.roll(ref[high, :].astype(F32), 64 * wz, 1)
            kept[span * s : span * s + span, :] = jnp.concatenate(
                [ref[low, :].astype(F32), upper[:, :64]], axis=1
            )

    def attend():
        return mm(held[...].astype(BF16), wp[...]).astype(BF16).astype(F32)

    def join(attended):
        middle = (kept[...] + gain1[...] * norm(attended, 1e-05)).astype(BF16)
        return middle, mm(middle, w_in[...])

    def feed(hidden):
        twice = (hidden * (1.0 + lax.erf(hidden * (1.0 / math.sqrt(2.0))))).astype(BF16)
        return mm(twice, w_out[...])

    def finish(middle, reduced2):
        result = (middle.astype(F32) + gain2[...] * norm(reduced2, 4e-05)).astype(BF16)
        before = (step + 8 // TYPES - 1) % (8 // TYPES)
        for s in range(2):
            done[s, pl.ds(pl.multiple_of(before * span, span), span), :] = result[span * s : span * s + span]

    @pl.when(step == 0)
    def _():
        scores, values = score(*project())
        weights = soften(scores)
        keep([mm(v, w) for v, w in zip(values, weights)])

    @pl.when((step > 0) & (step < steps))
    def _():
        attended = attend()
        projected = project()
        middle, hidden = join(attended)
        scores, values = score(*projected)
        reduced2 = feed(hidden)
        weights = soften(scores)
        mixes = [mm(v, w) for v, w in zip(values, weights)]
        finish(middle, reduced2)
        keep(mixes)

    @pl.when(step == steps)
    def _():
        middle, hidden = join(attend())
        finish(middle, feed(hidden))

    @pl.when((step == steps // 2) | (step == steps))
    def _():
        for half in range(2):
            for j in range(3):
                pairs = TILE_PAIRS[j]
                if j == 0:
                    rows = jnp.concatenate([done[half, 432:576, :], done[half, 0:288, :]], axis=0)
                else:
                    rows = done[half, 144 * pairs[0] : 144 * pairs[0] + 288, :]
                back = mm(unmat[j, :, : 144 * len(pairs)], rows).astype(BF16)
                for c in range(6):
                    for level in range(2):
                        k = 2 * c + level
                        z = lax.rem(2 * step // (steps // 2) + 3 + level, 4)
                        out[z, 6 * half + c, 16 * j : 16 * j + 16, :] = back[16 * k : 16 * k + 16]


def shifted_by(value, axis, steps):
    count = lax.axis_size(axis)
    return lax.ppermute(value, axis, [(i, (i + steps) % count) for i in range(count)])


def per_device(
    tokens, qkv_weight, proj_weight, bias_table, bias_index, norm_gain1, norm_gain2, mlp_in, mlp_out
):
    levels, lat, strip, channels = tokens.shape
    types, heads, count = bias_table.shape
    tok = tokens.transpose(0, 2, 1, 3)
    vmem = pl.BlockSpec(memory_space=pltpu.VMEM)
    send_shape = jax.ShapeDtypeStruct((types * GROUP * 3 // 2, 128), BF16)

    send_w, send_e = pl.pallas_call(
        pack_kernel,
        out_shape=(send_shape, send_shape),
        in_specs=[vmem] * 2,
        out_specs=(vmem,) * 2,
        name="pack",
    )(tok, jnp.asarray(pack_matrices(), BF16))
    halo_w = shifted_by(send_e, "lon", 1)
    table = bias_table.transpose(1, 0, 2).reshape(heads * types, count)
    tables, weight, w_out = pl.pallas_call(
        gather_kernel,
        out_shape=(
            jax.ShapeDtypeStruct((7, LANES // 128, 384, 128), F32),
            jax.ShapeDtypeStruct((2, 256, 768), BF16),
            jax.ShapeDtypeStruct(mlp_out.shape, BF16),
        ),
        in_specs=[vmem] * 4,
        out_specs=(vmem,) * 3,
        scratch_shapes=[
            pltpu.VMEM((3328, 128), F32),
            pltpu.VMEM((12, 4, GROUP, 128), F32),
            pltpu.VMEM((24, 144), jnp.int32),
            pltpu.SMEM((24, 144), jnp.int32),
            pltpu.SemaphoreType.DMA,
        ],
        compiler_params=pltpu.CompilerParams(vmem_limit_bytes=16 * 1024 * 1024),
        cost_estimate=pl.CostEstimate(flops=6_000_000_000, bytes_accessed=4_000_000, transcendentals=0),
        name="bias_gather",
    )(table, bias_index, qkv_weight, mlp_out.T)
    halo_e = shifted_by(send_w, "lon", -1)
    out = pl.pallas_call(
        main_kernel,
        grid=(types // TYPES + 1,),
        out_shape=jax.ShapeDtypeStruct((levels, strip, lat, channels), BF16),
        in_specs=[vmem] * 13,
        out_specs=vmem,
        scratch_shapes=[
            pltpu.VMEM((2, 576, channels), BF16),
            pltpu.VMEM((2 * TYPES * GROUP, channels), F32),
            pltpu.VMEM((2 * TYPES * GROUP, channels), F32),
        ],
        compiler_params=pltpu.CompilerParams(vmem_limit_bytes=32 * 1024 * 1024),
        name="block",
    )(
        send_w,
        send_e,
        halo_w,
        halo_e,
        tables,
        jnp.asarray(mask_codes(), jnp.int32),
        weight,
        proj_weight,
        norm_gain1[None],
        norm_gain2[None],
        mlp_in,
        w_out,
        jnp.asarray(unpack_matrices(), BF16),
    )
    return out.transpose(0, 2, 1, 3)


def solution(mesh):
    placed = (P("grp", None, "lon", None), P(), P(), P(), P(), P(), P(), P(), P())
    return jax.shard_map(
        per_device,
        mesh=mesh,
        in_specs=placed,
        out_specs=P("grp", None, "lon", None),
        check_vma=False,
    )
```

```python
import math

import jax
import jax.numpy as jnp
import numpy as np
from jax import lax
from jax.experimental import pallas as pl
from jax.experimental.pallas import tpu as pltpu
from jax.sharding import PartitionSpec as P

LOG2E = math.log2(math.e)
NEG = -1.0e9 * LOG2E
NT = (((1,), (1,)), ((), ()))
NN = (((1,), (0,)), ((), ()))
HEADS = 6
GROUP = 72
TYPES = 4
LANES = 512
F32 = jnp.float32
BF16 = jnp.bfloat16


def mm(a, b, dims=NN):
    return lax.dot_general(a, b, dims, preferred_element_type=F32)


PAIR_TILES = ((0,), (0, 1), (1, 2), (2, 0))
TILE_PAIRS = ((3, 0, 1), (1, 2), (2, 3))


def pair_rows(pair):
    out = []
    for w in range(2):
        for slot in range(12):
            for r in range(6):
                out.append((slot, (6 * (2 * pair + w) + r + 3) % 48))
    return out


def pack_matrices():
    mats = []
    for pair in range(4):
        for tile in PAIR_TILES[pair]:
            m = np.zeros((144, 192), np.float32)
            for k, (slot, a) in enumerate(pair_rows(pair)):
                if a // 16 == tile:
                    m[k, slot * 16 + a % 16] = 1.0
            mats.append(m)
    return np.stack(mats)


def unpack_matrices():
    mats = []
    for tile in range(3):
        pairs = TILE_PAIRS[tile]
        m = np.zeros((192, 144 * len(pairs)), np.float32)
        for n, pair in enumerate(pairs):
            for k, (slot, a) in enumerate(pair_rows(pair)):
                if a // 16 == tile:
                    m[slot * 16 + a % 16, 144 * n + k] = 1.0
        mats.append(np.pad(m, ((0, 0), (0, 432 - m.shape[1]))))
    return np.stack(mats)


def mask_codes():
    lane = np.arange(256)[None] + np.zeros((24, 1), np.int32)
    second = np.arange(24)[:, None] >= 12
    kr = np.arange(24)[:, None] % 12
    slot = (lane % GROUP) % 12
    code = ((slot >= 6) != (kr >= 6)) * 1 + ((slot % 6 >= 3) != (kr % 6 >= 3)) * 2
    source = np.where(second, (lane + 244) % 256, lane)
    place = np.where(source < 3 * GROUP, source % GROUP, GROUP) + 12 * second
    return np.stack([code, place])


def pack_kernel(tok, mats, send_w, send_e):
    for wz in range(2):
        zs = ((2 * wz + 1) % 4, (2 * wz + 2) % 4)
        for half, send in ((0, send_w), (1, send_e)):
            tiles = [
                jnp.concatenate(
                    [tok[z, 6 * half + c, 16 * j : 16 * j + 16, :] for c in range(6) for z in zs], axis=0
                )
                for j in range(3)
            ]
            at = 0
            for pair in range(4):
                total = None
                for j in PAIR_TILES[pair]:
                    part = mm(mats[at], tiles[j])
                    total = part if total is None else total + part
                    at += 1
                piece = total.astype(BF16)
                first = 576 * wz + 144 * pair
                send[first : first + 144, :] = piece[:, :128]
                send[1152 + 144 * pair : 1296 + 144 * pair, 64 * wz : 64 * wz + 64] = piece[:, 128:]


def turn(x, by):
    half = LANES // 2
    if by % half == 0:
        return x
    return jnp.concatenate([pltpu.roll(x[:, k : k + half], by % half, 1) for k in range(0, x.shape[1], half)], axis=1)


def gather_kernel(tab, index, qkv, mlp_out_t, codes, bias, weight, w_out, tables, tab_t, rows, picked, idx, sem):
    numbers = index[...].astype(F32)
    turned = numbers.T
    picked[...] = jnp.concatenate(
        [numbers[12 * e : 12 * e + 1] for e in range(12)] + [turned[12 * e : 12 * e + 1] for e in range(12)], axis=0
    ).astype(jnp.int32)
    copy = pltpu.make_async_copy(picked, idx, sem)
    copy.start()
    w_out[...] = mlp_out_t[...].astype(F32).T.astype(BF16)
    whole = qkv[...].astype(F32)
    gap = jnp.zeros((192, 32), F32)
    cols = []
    for k in range(6):
        cols += [whole[:, 96 * k : 96 * k + 96], gap]
    wide = jnp.concatenate(cols, axis=1).astype(BF16)
    none = jnp.zeros((64, 768), BF16)
    for wz in range(2):
        weight[wz, 0:128, :] = wide[:128]
        weight[wz, 128 + 64 * wz : 192 + 64 * wz, :] = wide[128:]
        weight[wz, 192 - 64 * wz : 256 - 64 * wz, :] = none
    count = tab.shape[1]
    for k in range(0, count, 128):
        n = min(128, count - k)
        tab_t[k : k + n, 0:96] = (tab[:, k : k + n] * LOG2E).T
    copy.wait()
    gap = jnp.zeros((16, 40), F32)
    for kr in range(12):
        j0 = kr * 12
        for m in range(4):
            for c in range(6):
                if m == 0:
                    cq, ck = 0, (12 - c if c else 11)
                elif m == 1:
                    cq, ck = 0, 6 - c
                else:
                    cq, ck = 6 * (m - 2) + c, 0
                for e in range(12):
                    r = idx[e, j0 + ck] if m < 2 else idx[12 + kr, e * 12 + cq]
                    rows[kr, m, c * 12 + e : c * 12 + e + 1, :] = tab_t[pl.ds(r, 1), :]
            t = rows[kr, m].T
            x = jnp.concatenate(
                [t[16 * h : 16 * h + 16, :] for h in range(3)]
                + [gap]
                + [t[16 * h : 16 * h + 16, :] for h in range(3, 6)]
                + [gap],
                axis=1,
            )
            for k in range(LANES // 128):
                tables[m, k, 16 * kr : 16 * kr + 16, :] = x[:, 128 * k : 128 * k + 128]


    def variants(kr, carry):
        here = pl.ds(pl.multiple_of(16 * kr, 16), 16)
        later = pl.ds(pl.multiple_of(192 + 16 * kr, 16), 16)
        for m in range(4):
            x = jnp.concatenate([tables[m, k, here, :] for k in range(LANES // 128)], axis=1)
            moved = turn(x, -GROUP)
            pieces = [(m, later, turn(x, 12))]
            if m < 3:
                pieces += [(4 + m, here, moved), (4 + m, later, turn(moved, 12))]
            for n, at, value in pieces:
                for k in range(LANES // 128):
                    tables[n, k, at, :] = value[:, 128 * k : 128 * k + 128]
        return carry

    lax.fori_loop(0, 12, variants, 0)
    place = jnp.concatenate([codes[1], codes[1]], axis=1)

    def widen(t, carry):
        mine = [
            jnp.concatenate([tables[m, k, pl.ds(t, 24, stride=16), :] for k in range(LANES // 128)], axis=1)
            for m in range(7)
        ]
        for s in range(2):
            for c in range(6):
                u, v = divmod(2 * c, 6)
                m = 3 - s - u
                first = pl.multiple_of(t * 288 + s * 144 + 24 * c, 8)
                bias[pl.ds(first, 24), :] = turn(jnp.where(place < GROUP - 12 * v, mine[m], mine[3 + m]), 12 * v)
        return carry

    lax.fori_loop(0, 16, widen, 0)


def norm(values, eps):
    average = jnp.mean(values, axis=-1, keepdims=True)
    centred = values - average
    spread = jnp.mean(centred * centred, axis=-1, keepdims=True)
    return centred * lax.rsqrt(spread + eps)


def main_kernel(
    send_w, send_e, halo_w, halo_e, bias, codes, weight, wp, gain1, gain2, w_in, w_out, unmat, out, done, held, kept
):
    step = pl.program_id(0)
    steps = 16 // TYPES
    span = TYPES * GROUP
    wz = step * TYPES // 8
    turn_of = step % (8 // TYPES)
    low = pl.ds(pl.multiple_of(step * span, span), span)
    high = pl.ds(pl.multiple_of(1152 + turn_of * span, span), span)
    sides = ((send_w, halo_w), (send_e, halo_e))

    def project():
        channel = lax.broadcasted_iota(jnp.int32, (1, 128), 1)
        scale = LOG2E / math.sqrt(32.0)
        heads = [jnp.where((channel >= 32 * i) & (channel < 32 * i + 32), scale, 0.0) for i in range(3)]
        own, halo = (
            jnp.concatenate([jnp.concatenate([s[k][low, :], s[k][high, :]], axis=1) for s in sides], axis=0)
            for k in range(2)
        )
        return heads, mm(own, weight[wz]), mm(halo, weight[wz, :, 256:])

    chains = [(s, t) for s in range(2) for t in range(TYPES)]

    def queries_of(heads, own_qkv):
        out = []
        for s, t in chains:
            at = span * s + GROUP * t
            for g in range(2):
                q = own_qkv[at : at + GROUP, 128 * g : 128 * g + 128]
                blocks = [q * heads[i] for i in range(3)] + [jnp.zeros((40, 128), F32)]
                out.append(jnp.concatenate(blocks, axis=0).astype(BF16))
        return out

    def windows(own_qkv, halo_kv, lanes):
        out = []
        for s, t in chains:
            at = span * s + GROUP * t
            parts = [own_qkv[at : at + GROUP, 256:][:, lanes], halo_kv[at : at + GROUP, lanes]]
            out.append(jnp.concatenate(parts[::-1] if s == 0 else parts, axis=0))
        return out

    def score(keys, queries):
        out = []
        for n, (s, t) in enumerate(chains):
            flags = jnp.where(wz == 1, 1, 0) + (jnp.where(turn_of == 8 // TYPES - 1, 2, 0) if t == TYPES - 1 else 0)
            bad = (codes[0] & flags) != 0
            for g in range(2):
                raw = mm(keys[n][:, 128 * g : 128 * g + 128], queries[2 * n + g], NT)
                chunks = []
                for k in range(6):
                    first = pl.multiple_of((step * TYPES + t) * 288 + s * 144 + 24 * k, 8)
                    offset = bias[pl.ds(first, 24), 256 * g : 256 * g + 256]
                    chunks.append(jnp.where(bad, NEG, raw[24 * k : 24 * k + 24] + offset))
                out.append(jnp.concatenate(chunks, axis=0))
        return out

    def soften(scores):
        return [jnp.exp2(x - jnp.max(x, axis=0, keepdims=True)).astype(BF16) for x in scores]

    def mix(turned, weights):
        ones = jnp.ones((16, 144), BF16)
        return [
            mm(jnp.concatenate([turned[n // 2][128 * (n % 2) : 128 * (n % 2) + 96], ones], axis=0), weights[n])
            for n in range(4 * TYPES)
        ]

    def keep(mixes):
        scaled = []
        for mixed in mixes:
            inverse = 1.0 / mixed[96:97]
            scaled.append([mixed[32 * i : 32 * i + 32] * inverse for i in range(3)])
        moved = [
            jnp.concatenate([p[i][:, GROUP * i : GROUP * i + GROUP] for i in range(3)], axis=0) for p in scaled
        ]
        for n in range(2 * TYPES):
            held[GROUP * n : GROUP * n + GROUP, :] = jnp.concatenate(moved[2 * n : 2 * n + 2], axis=0).T
        for s in range(2):
            ref = sides[s][0]
            upper = pltpu.roll(ref[high, :].astype(F32), 64 * wz, 1)
            kept[span * s : span * s + span, :] = jnp.concatenate(
                [ref[low, :].astype(F32), upper[:, :64]], axis=1
            )

    def attend():
        return mm(held[...].astype(BF16), wp[...])

    def join(attended):
        middle = kept[...] + gain1[...] * norm(attended, 1e-05)
        return middle, mm(middle.astype(BF16), w_in[...])

    def feed(hidden):
        twice = (hidden * (1.0 + lax.erf(hidden * (1.0 / math.sqrt(2.0))))).astype(BF16)
        return mm(twice, w_out[...])

    def finish(middle, reduced2):
        result = (middle + gain2[...] * norm(reduced2, 4e-05)).astype(BF16)
        before = (step + 8 // TYPES - 1) % (8 // TYPES)
        for s in range(2):
            done[s, pl.ds(pl.multiple_of(before * span, span), span), :] = result[span * s : span * s + span]

    keyed, valued = slice(0, 256), slice(256, 512)

    @pl.when(step == 0)
    def _():
        heads, own_qkv, halo_kv = project()
        keys = [x.astype(BF16) for x in windows(own_qkv, halo_kv, keyed)]
        scores = score(keys, queries_of(heads, own_qkv))
        turned = [x.T.astype(BF16) for x in windows(own_qkv, halo_kv, valued)]
        keep(mix(turned, soften(scores)))

    @pl.when((step > 0) & (step < steps))
    def _():
        attended = attend()
        heads, own_qkv, halo_kv = project()
        middle, hidden = join(attended)
        reduced2 = feed(hidden)
        keys = [x.astype(BF16) for x in windows(own_qkv, halo_kv, keyed)]
        queries = queries_of(heads, own_qkv)
        scores = score(keys, queries)
        turned = [x.T.astype(BF16) for x in windows(own_qkv, halo_kv, valued)]
        weights = soften(scores)
        mixes = mix(turned, weights)
        finish(middle, reduced2)
        keep(mixes)

    @pl.when(step == steps)
    def _():
        middle, hidden = join(attend())
        finish(middle, feed(hidden))

    @pl.when((step == steps // 2) | (step == steps))
    def _():
        for half in range(2):
            for j in range(3):
                pairs = TILE_PAIRS[j]
                if j == 0:
                    rows = jnp.concatenate([done[half, 432:576, :], done[half, 0:288, :]], axis=0)
                else:
                    rows = done[half, 144 * pairs[0] : 144 * pairs[0] + 288, :]
                back = mm(unmat[j, :, : 144 * len(pairs)], rows).astype(BF16)
                for c in range(6):
                    for level in range(2):
                        k = 2 * c + level
                        z = lax.rem(2 * step // (steps // 2) + 3 + level, 4)
                        out[z, 6 * half + c, 16 * j : 16 * j + 16, :] = back[16 * k : 16 * k + 16]


def shifted_by(value, axis, steps):
    count = lax.axis_size(axis)
    return lax.ppermute(value, axis, [(i, (i + steps) % count) for i in range(count)])


def per_device(
    tokens, qkv_weight, proj_weight, bias_table, bias_index, norm_gain1, norm_gain2, mlp_in, mlp_out
):
    levels, lat, strip, channels = tokens.shape
    types, heads, count = bias_table.shape
    tok = tokens.transpose(0, 2, 1, 3)
    vmem = pl.BlockSpec(memory_space=pltpu.VMEM)
    send_shape = jax.ShapeDtypeStruct((types * GROUP * 3 // 2, 128), BF16)

    send_w, send_e = pl.pallas_call(
        pack_kernel,
        out_shape=(send_shape, send_shape),
        in_specs=[vmem] * 2,
        out_specs=(vmem,) * 2,
        name="pack",
    )(tok, jnp.asarray(pack_matrices(), BF16))
    halo_w = shifted_by(send_e, "lon", 1)
    codes = jnp.asarray(mask_codes(), jnp.int32)
    table = bias_table.transpose(1, 0, 2).reshape(heads * types, count)
    bias, weight, w_out = pl.pallas_call(
        gather_kernel,
        out_shape=(
            jax.ShapeDtypeStruct((types * 288, LANES), F32),
            jax.ShapeDtypeStruct((2, 256, 768), BF16),
            jax.ShapeDtypeStruct(mlp_out.shape, BF16),
        ),
        in_specs=[vmem] * 5,
        out_specs=(vmem,) * 3,
        scratch_shapes=[
            pltpu.VMEM((7, LANES // 128, 384, 128), F32),
            pltpu.VMEM((3328, 128), F32),
            pltpu.VMEM((12, 4, GROUP, 128), F32),
            pltpu.VMEM((24, 144), jnp.int32),
            pltpu.SMEM((24, 144), jnp.int32),
            pltpu.SemaphoreType.DMA,
        ],
        compiler_params=pltpu.CompilerParams(vmem_limit_bytes=16 * 1024 * 1024),
        cost_estimate=pl.CostEstimate(flops=6_000_000_000, bytes_accessed=4_000_000, transcendentals=0),
        name="bias_gather",
    )(table, bias_index, qkv_weight, mlp_out.T, codes)
    halo_e = shifted_by(send_w, "lon", -1)
    out = pl.pallas_call(
        main_kernel,
        grid=(types // TYPES + 1,),
        out_shape=jax.ShapeDtypeStruct((levels, strip, lat, channels), BF16),
        in_specs=[vmem] * 13,
        out_specs=vmem,
        scratch_shapes=[
            pltpu.VMEM((2, 576, channels), BF16),
            pltpu.VMEM((2 * TYPES * GROUP, channels), F32),
            pltpu.VMEM((2 * TYPES * GROUP, channels), F32),
        ],
        compiler_params=pltpu.CompilerParams(vmem_limit_bytes=16 * 1024 * 1024),
        name="block",
    )(
        send_w,
        send_e,
        halo_w,
        halo_e,
        bias,
        codes,
        weight,
        proj_weight,
        norm_gain1[None],
        norm_gain2[None],
        mlp_in,
        w_out,
        jnp.asarray(unpack_matrices(), BF16),
    )
    return out.transpose(0, 2, 1, 3)


def solution(mesh):
    placed = (P("grp", None, "lon", None), P(), P(), P(), P(), P(), P(), P(), P())
    return jax.shard_map(
        per_device,
        mesh=mesh,
        in_specs=placed,
        out_specs=P("grp", None, "lon", None),
        check_vma=False,
    )
```

```python
import math

import jax
import jax.numpy as jnp
import numpy as np
from jax import lax
from jax.experimental import pallas as pl
from jax.experimental.pallas import tpu as pltpu
from jax.sharding import PartitionSpec as P

LOG2E = math.log2(math.e)
NEG = -1.0e9 * LOG2E
NT = (((1,), (1,)), ((), ()))
NN = (((1,), (0,)), ((), ()))
HEADS = 6
GROUP = 72
TYPES = 8
LANES = 512
F32 = jnp.float32
BF16 = jnp.bfloat16


def mm(a, b, dims=NN):
    return lax.dot_general(a, b, dims, preferred_element_type=F32)


PAIR_TILES = ((0,), (0, 1), (1, 2), (2, 0))
TILE_PAIRS = ((3, 0, 1), (1, 2), (2, 3))


def pair_rows(pair):
    out = []
    for w in range(2):
        for slot in range(12):
            for r in range(6):
                out.append((slot, (6 * (2 * pair + w) + r + 3) % 48))
    return out


def pack_matrices():
    mats = []
    for pair in range(4):
        for tile in PAIR_TILES[pair]:
            m = np.zeros((144, 192), np.float32)
            for k, (slot, a) in enumerate(pair_rows(pair)):
                if a // 16 == tile:
                    m[k, slot * 16 + a % 16] = 1.0
            mats.append(m)
    return np.stack(mats)


def unpack_matrices():
    mats = []
    for tile in range(3):
        pairs = TILE_PAIRS[tile]
        m = np.zeros((192, 144 * len(pairs)), np.float32)
        for n, pair in enumerate(pairs):
            for k, (slot, a) in enumerate(pair_rows(pair)):
                if a // 16 == tile:
                    m[slot * 16 + a % 16, 144 * n + k] = 1.0
        mats.append(np.pad(m, ((0, 0), (0, 432 - m.shape[1]))))
    return np.stack(mats)


def mask_codes():
    lane = np.arange(256)[None] + np.zeros((24, 1), np.int32)
    second = np.arange(24)[:, None] >= 12
    kr = np.arange(24)[:, None] % 12
    slot = (lane % GROUP) % 12
    code = ((slot >= 6) != (kr >= 6)) * 1 + ((slot % 6 >= 3) != (kr % 6 >= 3)) * 2
    source = np.where(second, (lane + 244) % 256, lane)
    place = np.where(source < 3 * GROUP, source % GROUP, GROUP) + 12 * second
    return np.stack([code, place])


def pack_kernel(tok, mats, send_w, send_e):
    for wz in range(2):
        zs = ((2 * wz + 1) % 4, (2 * wz + 2) % 4)
        for half, send in ((0, send_w), (1, send_e)):
            tiles = [
                jnp.concatenate(
                    [tok[z, 6 * half + c, 16 * j : 16 * j + 16, :] for c in range(6) for z in zs], axis=0
                )
                for j in range(3)
            ]
            at = 0
            for pair in range(4):
                total = None
                for j in PAIR_TILES[pair]:
                    part = mm(mats[at], tiles[j])
                    total = part if total is None else total + part
                    at += 1
                piece = total.astype(BF16)
                first = 576 * wz + 144 * pair
                send[first : first + 144, :] = piece[:, :128]
                send[1152 + 144 * pair : 1296 + 144 * pair, 64 * wz : 64 * wz + 64] = piece[:, 128:]


def turn(x, by):
    half = LANES // 2
    if by % half == 0:
        return x
    return jnp.concatenate([pltpu.roll(x[:, k : k + half], by % half, 1) for k in range(0, x.shape[1], half)], axis=1)


def gather_kernel(tab, index, qkv, mlp_out_t, codes, bias, weight, w_out, tables, tab_t, rows, picked, idx, sem):
    numbers = index[...].astype(F32)
    turned = numbers.T
    picked[...] = jnp.concatenate(
        [numbers[12 * e : 12 * e + 1] for e in range(12)] + [turned[12 * e : 12 * e + 1] for e in range(12)], axis=0
    ).astype(jnp.int32)
    copy = pltpu.make_async_copy(picked, idx, sem)
    copy.start()
    w_out[...] = mlp_out_t[...].astype(F32).T.astype(BF16)
    whole = qkv[...].astype(F32)
    gap = jnp.zeros((192, 32), F32)
    cols = []
    for k in range(6):
        cols += [whole[:, 96 * k : 96 * k + 96], gap]
    wide = jnp.concatenate(cols, axis=1).astype(BF16)
    none = jnp.zeros((64, 768), BF16)
    for wz in range(2):
        weight[wz, 0:128, :] = wide[:128]
        weight[wz, 128 + 64 * wz : 192 + 64 * wz, :] = wide[128:]
        weight[wz, 192 - 64 * wz : 256 - 64 * wz, :] = none
    count = tab.shape[1]
    for k in range(0, count, 128):
        n = min(128, count - k)
        tab_t[k : k + n, 0:96] = (tab[:, k : k + n] * LOG2E).T
    copy.wait()
    gap = jnp.zeros((16, 40), F32)
    for kr in range(12):
        j0 = kr * 12
        for m in range(4):
            for c in range(6):
                if m == 0:
                    cq, ck = 0, (12 - c if c else 11)
                elif m == 1:
                    cq, ck = 0, 6 - c
                else:
                    cq, ck = 6 * (m - 2) + c, 0
                for e in range(12):
                    r = idx[e, j0 + ck] if m < 2 else idx[12 + kr, e * 12 + cq]
                    rows[kr, m, c * 12 + e : c * 12 + e + 1, :] = tab_t[pl.ds(r, 1), :]
            t = rows[kr, m].T
            x = jnp.concatenate(
                [t[16 * h : 16 * h + 16, :] for h in range(3)]
                + [gap]
                + [t[16 * h : 16 * h + 16, :] for h in range(3, 6)]
                + [gap],
                axis=1,
            )
            for k in range(LANES // 128):
                tables[m, k, 16 * kr : 16 * kr + 16, :] = x[:, 128 * k : 128 * k + 128]


    def variants(kr, carry):
        here = pl.ds(pl.multiple_of(16 * kr, 16), 16)
        later = pl.ds(pl.multiple_of(192 + 16 * kr, 16), 16)
        for m in range(4):
            x = jnp.concatenate([tables[m, k, here, :] for k in range(LANES // 128)], axis=1)
            moved = turn(x, -GROUP)
            pieces = [(m, later, turn(x, 12))]
            if m < 3:
                pieces += [(4 + m, here, moved), (4 + m, later, turn(moved, 12))]
            for n, at, value in pieces:
                for k in range(LANES // 128):
                    tables[n, k, at, :] = value[:, 128 * k : 128 * k + 128]
        return carry

    lax.fori_loop(0, 12, variants, 0, unroll=4)
    place = jnp.concatenate([codes[1], codes[1]], axis=1)

    def widen(t, carry):
        mine = [
            jnp.concatenate([tables[m, k, pl.ds(t, 24, stride=16), :] for k in range(LANES // 128)], axis=1)
            for m in range(7)
        ]
        for s in range(2):
            for c in range(6):
                u, v = divmod(2 * c, 6)
                m = 3 - s - u
                first = pl.multiple_of(t * 288 + s * 144 + 24 * c, 8)
                bias[pl.ds(first, 24), :] = turn(jnp.where(place < GROUP - 12 * v, mine[m], mine[3 + m]), 12 * v)
        return carry

    lax.fori_loop(0, 16, widen, 0, unroll=8)


def norm(values, eps):
    average = jnp.mean(values, axis=-1, keepdims=True)
    centred = values - average
    spread = jnp.mean(centred * centred, axis=-1, keepdims=True)
    return centred * lax.rsqrt(spread + eps)


def main_kernel(
    send_w, send_e, halo_w, halo_e, bias, codes, weight, wp, gain1, gain2, w_in, w_out, unmat, out, done, held, kept
):
    step = pl.program_id(0)
    steps = 16 // TYPES
    span = TYPES * GROUP
    wz = step * TYPES // 8
    turn_of = step % (8 // TYPES)
    low = pl.ds(pl.multiple_of(step * span, span), span)
    high = pl.ds(pl.multiple_of(1152 + turn_of * span, span), span)
    sides = ((send_w, halo_w), (send_e, halo_e))

    def project():
        channel = lax.broadcasted_iota(jnp.int32, (1, 128), 1)
        scale = LOG2E / math.sqrt(32.0)
        heads = [jnp.where((channel >= 32 * i) & (channel < 32 * i + 32), scale, 0.0) for i in range(3)]
        own, halo = (
            jnp.concatenate([jnp.concatenate([s[k][low, :], s[k][high, :]], axis=1) for s in sides], axis=0)
            for k in range(2)
        )
        return heads, mm(own, weight[wz]), mm(halo, weight[wz, :, 256:])

    chains = [(s, t) for s in range(2) for t in range(TYPES)]

    def queries_of(heads, own_qkv):
        out = []
        for s, t in chains:
            at = span * s + GROUP * t
            for g in range(2):
                q = own_qkv[at : at + GROUP, 128 * g : 128 * g + 128]
                blocks = [q * heads[i] for i in range(3)] + [jnp.zeros((40, 128), F32)]
                out.append(jnp.concatenate(blocks, axis=0).astype(BF16))
        return out

    def windows(own_qkv, halo_kv, lanes):
        out = []
        for s, t in chains:
            at = span * s + GROUP * t
            parts = [own_qkv[at : at + GROUP, 256:][:, lanes], halo_kv[at : at + GROUP, lanes]]
            out.append(jnp.concatenate(parts[::-1] if s == 0 else parts, axis=0))
        return out

    def score(keys, queries):
        out = []
        for n, (s, t) in enumerate(chains):
            flags = jnp.where(wz == 1, 1, 0) + (jnp.where(turn_of == 8 // TYPES - 1, 2, 0) if t == TYPES - 1 else 0)
            bad = (codes[0] & flags) != 0
            for g in range(2):
                raw = mm(keys[n][:, 128 * g : 128 * g + 128], queries[2 * n + g], NT)
                chunks = []
                for k in range(6):
                    first = pl.multiple_of((step * TYPES + t) * 288 + s * 144 + 24 * k, 8)
                    offset = bias[pl.ds(first, 24), 256 * g : 256 * g + 256]
                    chunks.append(jnp.where(bad, NEG, raw[24 * k : 24 * k + 24] + offset))
                out.append(jnp.concatenate(chunks, axis=0))
        return out

    def soften(scores):
        return [jnp.exp2(x - jnp.max(x, axis=0, keepdims=True)).astype(BF16) for x in scores]

    def mix(turned, weights):
        ones = jnp.ones((16, 144), BF16)
        return [
            mm(jnp.concatenate([turned[n // 2][128 * (n % 2) : 128 * (n % 2) + 96], ones], axis=0), weights[n])
            for n in range(4 * TYPES)
        ]

    def keep(mixes):
        scaled = []
        for mixed in mixes:
            inverse = 1.0 / mixed[96:97]
            scaled.append([mixed[32 * i : 32 * i + 32] * inverse for i in range(3)])
        moved = [
            jnp.concatenate([p[i][:, GROUP * i : GROUP * i + GROUP] for i in range(3)], axis=0) for p in scaled
        ]
        for n in range(2 * TYPES):
            held[GROUP * n : GROUP * n + GROUP, :] = jnp.concatenate(moved[2 * n : 2 * n + 2], axis=0).T
        for s in range(2):
            ref = sides[s][0]
            upper = pltpu.roll(ref[high, :].astype(F32), 64 * wz, 1)
            kept[span * s : span * s + span, :] = jnp.concatenate(
                [ref[low, :].astype(F32), upper[:, :64]], axis=1
            )

    def attend():
        return mm(held[...].astype(BF16), wp[...])

    def join(attended):
        middle = kept[...] + gain1[...] * norm(attended, 1e-05)
        return middle, mm(middle.astype(BF16), w_in[...])

    def feed(hidden):
        twice = (hidden * (1.0 + lax.erf(hidden * (1.0 / math.sqrt(2.0))))).astype(BF16)
        return mm(twice, w_out[...])

    def finish(middle, reduced2):
        result = (middle + gain2[...] * norm(reduced2, 4e-05)).astype(BF16)
        before = (step + 8 // TYPES - 1) % (8 // TYPES)
        for s in range(2):
            done[s, pl.ds(pl.multiple_of(before * span, span), span), :] = result[span * s : span * s + span]

    keyed, valued = slice(0, 256), slice(256, 512)

    @pl.when(step == 0)
    def _():
        heads, own_qkv, halo_kv = project()
        keys = [x.astype(BF16) for x in windows(own_qkv, halo_kv, keyed)]
        scores = score(keys, queries_of(heads, own_qkv))
        turned = [x.T.astype(BF16) for x in windows(own_qkv, halo_kv, valued)]
        keep(mix(turned, soften(scores)))

    @pl.when((step > 0) & (step < steps))
    def _():
        attended = attend()
        heads, own_qkv, halo_kv = project()
        middle, hidden = join(attended)
        reduced2 = feed(hidden)
        keys = [x.astype(BF16) for x in windows(own_qkv, halo_kv, keyed)]
        queries = queries_of(heads, own_qkv)
        scores = score(keys, queries)
        turned = [x.T.astype(BF16) for x in windows(own_qkv, halo_kv, valued)]
        weights = soften(scores)
        mixes = mix(turned, weights)
        finish(middle, reduced2)
        keep(mixes)

    @pl.when(step == steps)
    def _():
        middle, hidden = join(attend())
        finish(middle, feed(hidden))

    @pl.when((step == steps // 2) | (step == steps))
    def _():
        for half in range(2):
            for j in range(3):
                pairs = TILE_PAIRS[j]
                if j == 0:
                    rows = jnp.concatenate([done[half, 432:576, :], done[half, 0:288, :]], axis=0)
                else:
                    rows = done[half, 144 * pairs[0] : 144 * pairs[0] + 288, :]
                back = mm(unmat[j, :, : 144 * len(pairs)], rows).astype(BF16)
                for c in range(6):
                    for level in range(2):
                        k = 2 * c + level
                        z = lax.rem(2 * step // (steps // 2) + 3 + level, 4)
                        out[z, 6 * half + c, 16 * j : 16 * j + 16, :] = back[16 * k : 16 * k + 16]


def shifted_by(value, axis, steps):
    count = lax.axis_size(axis)
    return lax.ppermute(value, axis, [(i, (i + steps) % count) for i in range(count)])


def per_device(
    tokens, qkv_weight, proj_weight, bias_table, bias_index, norm_gain1, norm_gain2, mlp_in, mlp_out
):
    levels, lat, strip, channels = tokens.shape
    types, heads, count = bias_table.shape
    tok = tokens.transpose(0, 2, 1, 3)
    vmem = pl.BlockSpec(memory_space=pltpu.VMEM)
    send_shape = jax.ShapeDtypeStruct((types * GROUP * 3 // 2, 128), BF16)

    send_w, send_e = pl.pallas_call(
        pack_kernel,
        out_shape=(send_shape, send_shape),
        in_specs=[vmem] * 2,
        out_specs=(vmem,) * 2,
        name="pack",
    )(tok, jnp.asarray(pack_matrices(), BF16))
    halo_w = shifted_by(send_e, "lon", 1)
    codes = jnp.asarray(mask_codes(), jnp.int32)
    table = bias_table.transpose(1, 0, 2).reshape(heads * types, count)
    bias, weight, w_out = pl.pallas_call(
        gather_kernel,
        out_shape=(
            jax.ShapeDtypeStruct((types * 288, LANES), F32),
            jax.ShapeDtypeStruct((2, 256, 768), BF16),
            jax.ShapeDtypeStruct(mlp_out.shape, BF16),
        ),
        in_specs=[vmem] * 5,
        out_specs=(vmem,) * 3,
        scratch_shapes=[
            pltpu.VMEM((7, LANES // 128, 384, 128), F32),
            pltpu.VMEM((3328, 128), F32),
            pltpu.VMEM((12, 4, GROUP, 128), F32),
            pltpu.VMEM((24, 144), jnp.int32),
            pltpu.SMEM((24, 144), jnp.int32),
            pltpu.SemaphoreType.DMA,
        ],
        compiler_params=pltpu.CompilerParams(vmem_limit_bytes=16 * 1024 * 1024),
        cost_estimate=pl.CostEstimate(flops=6_000_000_000, bytes_accessed=4_000_000, transcendentals=0),
        name="bias_gather",
    )(table, bias_index, qkv_weight, mlp_out.T, codes)
    halo_e = shifted_by(send_w, "lon", -1)
    out = pl.pallas_call(
        main_kernel,
        grid=(types // TYPES + 1,),
        out_shape=jax.ShapeDtypeStruct((levels, strip, lat, channels), BF16),
        in_specs=[vmem] * 13,
        out_specs=vmem,
        scratch_shapes=[
            pltpu.VMEM((2, 576, channels), BF16),
            pltpu.VMEM((2 * TYPES * GROUP, channels), F32),
            pltpu.VMEM((2 * TYPES * GROUP, channels), F32),
        ],
        compiler_params=pltpu.CompilerParams(vmem_limit_bytes=16 * 1024 * 1024),
        name="block",
    )(
        send_w,
        send_e,
        halo_w,
        halo_e,
        bias,
        codes,
        weight,
        proj_weight,
        norm_gain1[None],
        norm_gain2[None],
        mlp_in,
        w_out,
        jnp.asarray(unpack_matrices(), BF16),
    )
    return out.transpose(0, 2, 1, 3)


def solution(mesh):
    placed = (P("grp", None, "lon", None), P(), P(), P(), P(), P(), P(), P(), P())
    return jax.shard_map(
        per_device,
        mesh=mesh,
        in_specs=placed,
        out_specs=P("grp", None, "lon", None),
        check_vma=False,
    )
```

```python
import math

import jax
import jax.numpy as jnp
import numpy as np
from jax import lax
from jax.experimental import pallas as pl
from jax.experimental.pallas import tpu as pltpu
from jax.sharding import PartitionSpec as P

LOG2E = math.log2(math.e)
NEG = -1.0e9 * LOG2E
NT = (((1,), (1,)), ((), ()))
NN = (((1,), (0,)), ((), ()))
HEADS = 6
GROUP = 72
TYPES = 8
LANES = 512
F32 = jnp.float32
BF16 = jnp.bfloat16


def mm(a, b, dims=NN):
    return lax.dot_general(a, b, dims, preferred_element_type=F32)


PAIR_TILES = ((0,), (0, 1), (1, 2), (2, 0))
TILE_PAIRS = ((3, 0, 1), (1, 2), (2, 3))


def pair_rows(pair):
    out = []
    for w in range(2):
        for slot in range(12):
            for r in range(6):
                out.append((slot, (6 * (2 * pair + w) + r + 3) % 48))
    return out


def pack_matrices():
    mats = []
    for pair in range(4):
        for tile in PAIR_TILES[pair]:
            m = np.zeros((144, 192), np.float32)
            for k, (slot, a) in enumerate(pair_rows(pair)):
                if a // 16 == tile:
                    m[k, slot * 16 + a % 16] = 1.0
            mats.append(m)
    return np.stack(mats)


def unpack_matrices():
    mats = []
    for tile in range(3):
        pairs = TILE_PAIRS[tile]
        m = np.zeros((192, 144 * len(pairs)), np.float32)
        for n, pair in enumerate(pairs):
            for k, (slot, a) in enumerate(pair_rows(pair)):
                if a // 16 == tile:
                    m[slot * 16 + a % 16, 144 * n + k] = 1.0
        mats.append(np.pad(m, ((0, 0), (0, 432 - m.shape[1]))))
    return np.stack(mats)


def mask_codes():
    lane = np.arange(256)[None] + np.zeros((24, 1), np.int32)
    second = np.arange(24)[:, None] >= 12
    kr = np.arange(24)[:, None] % 12
    slot = (lane % GROUP) % 12
    code = ((slot >= 6) != (kr >= 6)) * 1 + ((slot % 6 >= 3) != (kr % 6 >= 3)) * 2
    source = np.where(second, (lane + 244) % 256, lane)
    place = np.where(source < 3 * GROUP, source % GROUP, GROUP) + 12 * second
    return np.stack([code, place])


def pack_kernel(tok, mats, index, qkv, send_w, send_e, picked, weight):
    for wz in range(2):
        zs = ((2 * wz + 1) % 4, (2 * wz + 2) % 4)
        for half, send in ((0, send_w), (1, send_e)):
            tiles = [
                jnp.concatenate(
                    [tok[z, 6 * half + c, 16 * j : 16 * j + 16, :] for c in range(6) for z in zs], axis=0
                )
                for j in range(3)
            ]
            at = 0
            for pair in range(4):
                total = None
                for j in PAIR_TILES[pair]:
                    part = mm(mats[at], tiles[j])
                    total = part if total is None else total + part
                    at += 1
                piece = total.astype(BF16)
                first = 576 * wz + 144 * pair
                send[first : first + 144, :] = piece[:, :128]
                send[1152 + 144 * pair : 1296 + 144 * pair, 64 * wz : 64 * wz + 64] = piece[:, 128:]
    numbers = index[...].astype(F32)
    turned = numbers.T
    picked[...] = jnp.concatenate(
        [numbers[12 * e : 12 * e + 1] for e in range(12)] + [turned[12 * e : 12 * e + 1] for e in range(12)], axis=0
    ).astype(jnp.int32)
    whole = qkv[...].astype(F32)
    gap = jnp.zeros((192, 32), F32)
    cols = []
    for k in range(6):
        cols += [whole[:, 96 * k : 96 * k + 96], gap]
    wide = jnp.concatenate(cols, axis=1).astype(BF16)
    none = jnp.zeros((64, 768), BF16)
    for wz in range(2):
        weight[wz, 0:128, :] = wide[:128]
        weight[wz, 128 + 64 * wz : 192 + 64 * wz, :] = wide[128:]
        weight[wz, 192 - 64 * wz : 256 - 64 * wz, :] = none


def turn(x, by):
    half = LANES // 2
    if by % half == 0:
        return x
    return jnp.concatenate([pltpu.roll(x[:, k : k + half], by % half, 1) for k in range(0, x.shape[1], half)], axis=1)


def gather_kernel(tab, picked, mlp_out_t, codes, bias, w_out, tables, tab_t, rows, idx, sem):
    copy = pltpu.make_async_copy(picked, idx, sem)
    copy.start()
    w_out[...] = mlp_out_t[...].astype(F32).T.astype(BF16)
    count = tab.shape[1]
    for k in range(0, count, 128):
        n = min(128, count - k)
        tab_t[k : k + n, 0:96] = (tab[:, k : k + n] * LOG2E).T
    copy.wait()
    gap = jnp.zeros((16, 40), F32)
    for kr in range(12):
        j0 = kr * 12
        for m in range(4):
            for c in range(6):
                if m == 0:
                    cq, ck = 0, (12 - c if c else 11)
                elif m == 1:
                    cq, ck = 0, 6 - c
                else:
                    cq, ck = 6 * (m - 2) + c, 0
                for e in range(12):
                    r = idx[e, j0 + ck] if m < 2 else idx[12 + kr, e * 12 + cq]
                    rows[kr, m, c * 12 + e : c * 12 + e + 1, :] = tab_t[pl.ds(r, 1), :]
            t = rows[kr, m].T
            x = jnp.concatenate(
                [t[16 * h : 16 * h + 16, :] for h in range(3)]
                + [gap]
                + [t[16 * h : 16 * h + 16, :] for h in range(3, 6)]
                + [gap],
                axis=1,
            )
            for k in range(LANES // 128):
                tables[m, k, 16 * kr : 16 * kr + 16, :] = x[:, 128 * k : 128 * k + 128]


    def variants(kr, carry):
        here = pl.ds(pl.multiple_of(16 * kr, 16), 16)
        later = pl.ds(pl.multiple_of(192 + 16 * kr, 16), 16)
        for m in range(4):
            x = jnp.concatenate([tables[m, k, here, :] for k in range(LANES // 128)], axis=1)
            moved = turn(x, -GROUP)
            pieces = [(m, later, turn(x, 12))]
            if m < 3:
                pieces += [(4 + m, here, moved), (4 + m, later, turn(moved, 12))]
            for n, at, value in pieces:
                for k in range(LANES // 128):
                    tables[n, k, at, :] = value[:, 128 * k : 128 * k + 128]
        return carry

    lax.fori_loop(0, 12, variants, 0, unroll=4)
    place = jnp.concatenate([codes[1], codes[1]], axis=1)

    def widen(t, carry):
        mine = [
            jnp.concatenate([tables[m, k, pl.ds(t, 24, stride=16), :] for k in range(LANES // 128)], axis=1)
            for m in range(7)
        ]
        for s in range(2):
            for c in range(6):
                u, v = divmod(2 * c, 6)
                m = 3 - s - u
                first = pl.multiple_of(t * 288 + s * 144 + 24 * c, 8)
                bias[pl.ds(first, 24), :] = turn(jnp.where(place < GROUP - 12 * v, mine[m], mine[3 + m]), 12 * v)
        return carry

    lax.fori_loop(0, 16, widen, 0, unroll=8)


def norm(values, eps):
    average = jnp.mean(values, axis=-1, keepdims=True)
    centred = values - average
    spread = jnp.mean(centred * centred, axis=-1, keepdims=True)
    return centred * lax.rsqrt(spread + eps)


def main_kernel(
    send_w, send_e, halo_w, halo_e, bias, codes, weight, wp, gain1, gain2, w_in, w_out, unmat, out, done, held, kept
):
    step = pl.program_id(0)
    steps = 16 // TYPES
    span = TYPES * GROUP
    wz = step * TYPES // 8
    turn_of = step % (8 // TYPES)
    low = pl.ds(pl.multiple_of(step * span, span), span)
    high = pl.ds(pl.multiple_of(1152 + turn_of * span, span), span)
    sides = ((send_w, halo_w), (send_e, halo_e))

    def project():
        channel = lax.broadcasted_iota(jnp.int32, (1, 128), 1)
        scale = LOG2E / math.sqrt(32.0)
        heads = [jnp.where((channel >= 32 * i) & (channel < 32 * i + 32), scale, 0.0) for i in range(3)]
        own, halo = (
            jnp.concatenate([jnp.concatenate([s[k][low, :], s[k][high, :]], axis=1) for s in sides], axis=0)
            for k in range(2)
        )
        return heads, mm(own, weight[wz]), mm(halo, weight[wz, :, 256:])

    chains = [(s, t) for s in range(2) for t in range(TYPES)]

    def queries_of(heads, own_qkv):
        out = []
        for s, t in chains:
            at = span * s + GROUP * t
            for g in range(2):
                q = own_qkv[at : at + GROUP, 128 * g : 128 * g + 128]
                blocks = [q * heads[i] for i in range(3)] + [jnp.zeros((40, 128), F32)]
                out.append(jnp.concatenate(blocks, axis=0).astype(BF16))
        return out

    def windows(own_qkv, halo_kv, lanes):
        out = []
        for s, t in chains:
            at = span * s + GROUP * t
            parts = [own_qkv[at : at + GROUP, 256:][:, lanes], halo_kv[at : at + GROUP, lanes]]
            out.append(jnp.concatenate(parts[::-1] if s == 0 else parts, axis=0))
        return out

    def score(keys, queries):
        out = []
        for n, (s, t) in enumerate(chains):
            flags = jnp.where(wz == 1, 1, 0) + (jnp.where(turn_of == 8 // TYPES - 1, 2, 0) if t == TYPES - 1 else 0)
            bad = (codes[0] & flags) != 0
            for g in range(2):
                raw = mm(keys[n][:, 128 * g : 128 * g + 128], queries[2 * n + g], NT)
                chunks = []
                for k in range(6):
                    first = pl.multiple_of((step * TYPES + t) * 288 + s * 144 + 24 * k, 8)
                    offset = bias[pl.ds(first, 24), 256 * g : 256 * g + 256]
                    chunks.append(jnp.where(bad, NEG, raw[24 * k : 24 * k + 24] + offset))
                out.append(jnp.concatenate(chunks, axis=0))
        return out

    def soften(scores):
        return [jnp.exp2(x - jnp.max(x, axis=0, keepdims=True)).astype(BF16) for x in scores]

    def mix(turned, weights):
        ones = jnp.ones((16, 144), BF16)
        return [
            mm(jnp.concatenate([turned[n // 2][128 * (n % 2) : 128 * (n % 2) + 96], ones], axis=0), weights[n])
            for n in range(4 * TYPES)
        ]

    def keep(mixes):
        scaled = []
        for mixed in mixes:
            inverse = 1.0 / mixed[96:97]
            scaled.append([mixed[32 * i : 32 * i + 32] * inverse for i in range(3)])
        moved = [
            jnp.concatenate([p[i][:, GROUP * i : GROUP * i + GROUP] for i in range(3)], axis=0) for p in scaled
        ]
        for n in range(2 * TYPES):
            held[GROUP * n : GROUP * n + GROUP, :] = jnp.concatenate(moved[2 * n : 2 * n + 2], axis=0).T
        for s in range(2):
            ref = sides[s][0]
            upper = pltpu.roll(ref[high, :].astype(F32), 64 * wz, 1)
            kept[span * s : span * s + span, :] = jnp.concatenate(
                [ref[low, :].astype(F32), upper[:, :64]], axis=1
            )

    def attend():
        return mm(held[...].astype(BF16), wp[...])

    def join(attended):
        middle = kept[...] + gain1[...] * norm(attended, 1e-05)
        return middle, mm(middle.astype(BF16), w_in[...])

    def feed(hidden):
        twice = (hidden * (1.0 + lax.erf(hidden * (1.0 / math.sqrt(2.0))))).astype(BF16)
        return mm(twice, w_out[...])

    def finish(middle, reduced2):
        result = (middle + gain2[...] * norm(reduced2, 4e-05)).astype(BF16)
        before = (step + 8 // TYPES - 1) % (8 // TYPES)
        for s in range(2):
            done[s, pl.ds(pl.multiple_of(before * span, span), span), :] = result[span * s : span * s + span]

    keyed, valued = slice(0, 256), slice(256, 512)

    @pl.when(step == 0)
    def _():
        heads, own_qkv, halo_kv = project()
        keys = [x.astype(BF16) for x in windows(own_qkv, halo_kv, keyed)]
        scores = score(keys, queries_of(heads, own_qkv))
        turned = [x.T.astype(BF16) for x in windows(own_qkv, halo_kv, valued)]
        keep(mix(turned, soften(scores)))

    @pl.when((step > 0) & (step < steps))
    def _():
        attended = attend()
        heads, own_qkv, halo_kv = project()
        middle, hidden = join(attended)
        reduced2 = feed(hidden)
        keys = [x.astype(BF16) for x in windows(own_qkv, halo_kv, keyed)]
        queries = queries_of(heads, own_qkv)
        scores = score(keys, queries)
        turned = [x.T.astype(BF16) for x in windows(own_qkv, halo_kv, valued)]
        weights = soften(scores)
        mixes = mix(turned, weights)
        finish(middle, reduced2)
        keep(mixes)

    @pl.when(step == steps)
    def _():
        middle, hidden = join(attend())
        finish(middle, feed(hidden))

    @pl.when((step == steps // 2) | (step == steps))
    def _():
        for half in range(2):
            for j in range(3):
                pairs = TILE_PAIRS[j]
                if j == 0:
                    rows = jnp.concatenate([done[half, 432:576, :], done[half, 0:288, :]], axis=0)
                else:
                    rows = done[half, 144 * pairs[0] : 144 * pairs[0] + 288, :]
                back = mm(unmat[j, :, : 144 * len(pairs)], rows).astype(BF16)
                for c in range(6):
                    for level in range(2):
                        k = 2 * c + level
                        z = lax.rem(2 * step // (steps // 2) + 3 + level, 4)
                        out[z, 6 * half + c, 16 * j : 16 * j + 16, :] = back[16 * k : 16 * k + 16]


def shifted_by(value, axis, steps):
    count = lax.axis_size(axis)
    return lax.ppermute(value, axis, [(i, (i + steps) % count) for i in range(count)])


def per_device(
    tokens, qkv_weight, proj_weight, bias_table, bias_index, norm_gain1, norm_gain2, mlp_in, mlp_out
):
    levels, lat, strip, channels = tokens.shape
    types, heads, count = bias_table.shape
    tok = tokens.transpose(0, 2, 1, 3)
    vmem = pl.BlockSpec(memory_space=pltpu.VMEM)
    send_shape = jax.ShapeDtypeStruct((types * GROUP * 3 // 2, 128), BF16)

    send_w, send_e, picked, weight = pl.pallas_call(
        pack_kernel,
        out_shape=(
            send_shape,
            send_shape,
            jax.ShapeDtypeStruct((24, 144), jnp.int32),
            jax.ShapeDtypeStruct((2, 256, 768), BF16),
        ),
        in_specs=[vmem] * 4,
        out_specs=(vmem,) * 4,
        name="pack",
    )(tok, jnp.asarray(pack_matrices(), BF16), bias_index, qkv_weight)
    halo_w = shifted_by(send_e, "lon", 1)
    codes = jnp.asarray(mask_codes(), jnp.int32)
    table = bias_table.transpose(1, 0, 2).reshape(heads * types, count)
    bias, w_out = pl.pallas_call(
        gather_kernel,
        out_shape=(
            jax.ShapeDtypeStruct((types * 288, LANES), F32),
            jax.ShapeDtypeStruct(mlp_out.shape, BF16),
        ),
        in_specs=[vmem] * 4,
        out_specs=(vmem,) * 2,
        scratch_shapes=[
            pltpu.VMEM((7, LANES // 128, 384, 128), F32),
            pltpu.VMEM((3328, 128), F32),
            pltpu.VMEM((12, 4, GROUP, 128), F32),
            pltpu.SMEM((24, 144), jnp.int32),
            pltpu.SemaphoreType.DMA,
        ],
        compiler_params=pltpu.CompilerParams(vmem_limit_bytes=16 * 1024 * 1024),
        cost_estimate=pl.CostEstimate(flops=6_000_000_000, bytes_accessed=4_000_000, transcendentals=0),
        name="bias_gather",
    )(table, picked, mlp_out.T, codes)
    halo_e = shifted_by(send_w, "lon", -1)
    out = pl.pallas_call(
        main_kernel,
        grid=(types // TYPES + 1,),
        out_shape=jax.ShapeDtypeStruct((levels, strip, lat, channels), BF16),
        in_specs=[vmem] * 13,
        out_specs=vmem,
        scratch_shapes=[
            pltpu.VMEM((2, 576, channels), BF16),
            pltpu.VMEM((2 * TYPES * GROUP, channels), F32),
            pltpu.VMEM((2 * TYPES * GROUP, channels), F32),
        ],
        compiler_params=pltpu.CompilerParams(vmem_limit_bytes=16 * 1024 * 1024),
        name="block",
    )(
        send_w,
        send_e,
        halo_w,
        halo_e,
        bias,
        codes,
        weight,
        proj_weight,
        norm_gain1[None],
        norm_gain2[None],
        mlp_in,
        w_out,
        jnp.asarray(unpack_matrices(), BF16),
    )
    return out.transpose(0, 2, 1, 3)


def solution(mesh):
    placed = (P("grp", None, "lon", None), P(), P(), P(), P(), P(), P(), P(), P())
    return jax.shard_map(
        per_device,
        mesh=mesh,
        in_specs=placed,
        out_specs=P("grp", None, "lon", None),
        check_vma=False,
    )
```
